512 devices in a mesh: dp: 8 (over x, z_hi), ep: 64 (over y, z_lo, core).
Axes of the slice: x: 4, y: 4, z: 16 (z_hi: 2, z_lo: 8; z = z_hi * 8 + z_lo), core: 2. Of those that a mesh axis runs over, the one named last changes fastest.
Arguments:
- trainer_weights: bfloat16 [64, 2, 1024, 2304], P('ep', None, 'dp'), may hold values from -0.125 to 0.125
- trainer_place: int32 [64], replicated, may hold values from 0 to 63, each once
- engine_place: int32 [64], replicated, may hold values from 0 to 63, each once
- tokens: bfloat16 [8192, 2048], P(('dp', 'ep')), may hold values from -6 to 6
- routes: int32 [8192, 8], P(('dp', 'ep')), may hold values from 0 to 63, all different within a row; in each aligned block of 16 rows (0 to 15, 16 to 31, ...) at most 4 rows name the same one
- gates: float32 [8192, 8], P(('dp', 'ep')), may hold values from 0.1 to 1
Outputs:
- mixed: bfloat16 [8192, 2048], P(('dp', 'ep'))
- slot_load: float32 [8, 64], P('dp', 'ep')
The draws below stay inside these ranges and needn't reach their ends.
Inputs may be any that keep to these rules, and one draw needn't show every extreme that they name: `trainer_place`: a permutation of 0 to 63. `engine_place`: a permutation of 0 to 63. `routes`: the 8 experts of a row differ; among the 16 rows of one device (aligned blocks of 16 rows) no expert is named by more than 4 rows, a bound that some block reaches.
All inputs are finite; a program needn't handle non-finite values.
Results may differ from the reference program's by a relative error of at most 0.0057.
Values may be sent and summed in bfloat16 or wider, within the bound.
A program may use at most 64 MiB of HBM per device.

```python
import math
import jax
import jax.numpy as jnp
import numpy as np
from jax import lax

D = 2048
FF = 768
TOP = 8
TOK_DEV = 16
E = 64
CAP = 4
ROWS = 8192
N_DP = 8
N_EP = 64


def steps_of(rng, dims, split, least, largest):
    def one(axis_at, parts):
        heights = jax.random.uniform(jax.random.fold_in(jax.random.fold_in(rng, 6), axis_at), (parts,), jnp.float32, least / len(split), largest / len(split))
        return jnp.repeat(jnp.exp(heights), dims[axis_at] // parts).reshape((-1,) + (1,) * (len(dims) - axis_at - 1))

    factor_of = one(*split[0])
    for cut in split[1:]:
        factor_of = factor_of * one(*cut)
    return factor_of


def routed_block(key, own, number, rows, count, top, bound, slope):
    ranking = jax.random.permutation(key, count)
    heavy_load, ordinary = portions_of(count, rows * top, bound, slope, True), portions_of(count, rows * top, bound, slope, False)
    places = jnp.arange(count)

    def named(lengths, rotation):
        used = int((lengths > 0).sum())
        fixed = max(1, used // 4)
        shifted = fixed + (places - fixed + rotation * (used - fixed)) % max(1, count - fixed)
        return jnp.zeros((count,), jnp.int32).at[ranking[jnp.where(places < fixed, places, shifted)]].set(jnp.asarray(lengths, jnp.int32))

    lengths = jnp.where(number % 4 == 0, named(heavy_load, number // 4), named(ordinary, number - number // 4 - 1))
    mixed = jax.random.permutation(jax.random.fold_in(own, 3), count)
    giver, taker = mixed[0:count // 2 * 2:2], mixed[1:count // 2 * 2:2]
    slack = jnp.minimum(lengths[giver] - 1, bound - lengths[taker]) // 2
    slack = jnp.where((giver == ranking[0]) | (taker == ranking[0]) | (lengths[taker] == 0), 0, jnp.maximum(slack, 0))
    shifted = jax.random.randint(jax.random.fold_in(own, 4), (count // 2,), 0, 1 << 20) % (slack + 1)
    lengths = lengths.at[giver].add(-shifted).at[taker].add(shifted)
    items = jnp.searchsorted(jnp.cumsum(lengths), jnp.arange(rows * top), side="right").astype(jnp.int32)
    grid = items.reshape(top, rows).T
    grid = grid[jax.random.permutation(jax.random.fold_in(own, 1), rows)]
    rotation = jax.random.randint(jax.random.fold_in(own, 2), (rows, 1), 0, top)
    return jnp.take_along_axis(grid, (jnp.arange(top)[None, :] + rotation) % top, axis=1)


def portions_of(count, total, bound, lean, full):
    loads = [(1 << 20) // math.isqrt(grade ** lean) + 1 for grade in range(1, count + 1)]
    largest = bound if full else min(bound, max(-(-total // count), total * loads[0] // sum(loads)))
    least = 1 if total - largest >= count - 1 else 0
    holding, rest = [largest] + [least] * (count - 1), total - largest - least * (count - 1)
    while rest > 0:
        movable = [i for i in range(1, count) if holding[i] < largest] or [i for i in range(1, count) if holding[i] < bound]
        mass, budget = sum([loads[i] for i in movable]), rest
        for i in movable:
            more = min(bound - holding[i], max(1, budget * loads[i] // mass), rest)
            holding[i] = holding[i] + more
            rest = rest - more
    return np.array(holding)


def gaussian(rng, extent, width, reach, cuts=(), kind=jnp.bfloat16):
    entries = jax.random.normal(rng, extent, jnp.float32) * width
    if len(cuts) > 0:
        entries = steps_of(rng, extent, cuts, -0.22, 0.18) * entries
    return jnp.clip(entries, min=-reach, max=reach).astype(kind)


def setup_inputs(seed: int = 0) -> dict:
    splits = jax.random.split(jax.random.key(seed), 7)
    trainer_weights = gaussian(splits[0], (N_EP, 2, D // 2, 3 * FF), D ** -0.5, 0.125, ((0, 64), (2, 8)))
    trainer_place = jax.random.permutation(splits[1], E).astype(jnp.int32)
    engine_place = jax.random.permutation(splits[2], E).astype(jnp.int32)
    tokens = gaussian(splits[3], (ROWS, D), 1.0, 6.0, ((0, 512),))
    routes_keys = jax.random.split(jax.random.fold_in(splits[4], 1), ROWS // TOK_DEV)
    routes_turns = jax.random.permutation(jax.random.fold_in(splits[4], 3), ROWS // TOK_DEV)
    routes = jax.vmap(lambda own, number: routed_block(jax.random.fold_in(splits[4], 2), own, number, TOK_DEV, E, TOP, CAP, 2))(routes_keys, routes_turns).reshape((ROWS, TOP))
    gates = jnp.clip(0.1 + 0.9 * jax.random.uniform(splits[5], (ROWS, TOP), jnp.float32) ** steps_of(splits[5], (ROWS, TOP), ((0, 512),), -0.2, 0.2), 0.1, 1.0)
    return dict(trainer_weights=trainer_weights, trainer_place=trainer_place, engine_place=engine_place, tokens=tokens, routes=routes, gates=gates)


block_rows = 256


def expert_rows(rows_in, weight):
    both = jnp.dot(rows_in, weight[:, :2 * FF], preferred_element_type=jnp.float32)
    hidden = (jax.nn.silu(both[:, :FF]) * both[:, FF:]).astype(jnp.bfloat16)
    result = lax.dot_general(hidden, weight[:, 2 * FF:], (((1,), (1,)), ((), ())), preferred_element_type=jnp.float32)
    return result.astype(jnp.bfloat16)


def slot_matrix(trainer_weights, slot):
    group = (slot // 2).astype(jnp.int32)
    local = (slot % 2).astype(jnp.int32)
    first = lax.dynamic_index_in_dim(trainer_weights, (2 * group).astype(jnp.int32), 0, keepdims=False)
    second = lax.dynamic_index_in_dim(trainer_weights, (2 * group + 1).astype(jnp.int32), 0, keepdims=False)
    upper = lax.dynamic_index_in_dim(first, local, 0, keepdims=False)
    lower = lax.dynamic_index_in_dim(second, local, 0, keepdims=False)
    return jnp.concatenate([upper, lower], axis=0)


def reference(trainer_weights, trainer_place, engine_place, tokens, routes, gates):
    flat_expert = routes.reshape(-1).astype(jnp.int32)
    sort_order = jnp.argsort(flat_expert, stable=True).astype(jnp.int32)
    sorted_token = (sort_order // TOP).astype(jnp.int32)
    sorted_gate = gates.reshape(-1)[sort_order]
    sorted_token = jnp.concatenate([sorted_token, jnp.zeros((block_rows,), jnp.int32)])
    sorted_gate = jnp.concatenate([sorted_gate, jnp.zeros((block_rows,), sorted_gate.dtype)])
    counts = jnp.bincount(flat_expert, length=E).astype(jnp.int32)
    starts = (jnp.cumsum(counts) - counts).astype(jnp.int32)
    expert_ids = jnp.arange(E, dtype=jnp.int32)
    slot_of = jnp.argmax(trainer_place[None, :] == expert_ids[:, None], axis=1).astype(jnp.int32)

    def per_expert(expert, mixed_sum):
        expert = jnp.asarray(expert).astype(jnp.int32)
        weight = slot_matrix(trainer_weights, slot_of[expert])
        count = counts[expert]
        begin = starts[expert]

        def per_block(block_index, inner):
            block_index = jnp.asarray(block_index).astype(jnp.int32)
            offset = (begin + block_index * block_rows).astype(jnp.int32)
            token_ids = lax.dynamic_slice_in_dim(sorted_token, offset, block_rows)
            block_gate = lax.dynamic_slice_in_dim(sorted_gate, offset, block_rows)
            valid = (block_index * block_rows + jnp.arange(block_rows, dtype=jnp.int32)) < count
            outputs = expert_rows(tokens[token_ids], weight).astype(jnp.float32)
            scaled = jnp.where(valid[:, None], outputs * block_gate[:, None], jnp.zeros_like(outputs))
            return inner.at[token_ids].add(scaled)

        blocks = ((count + block_rows - 1) // block_rows).astype(jnp.int32)
        return lax.fori_loop(jnp.int32(0), blocks, per_block, mixed_sum)

    mixed_sum = lax.fori_loop(0, E, per_expert, jnp.zeros((ROWS, D), jnp.float32))
    per_replica = routes.reshape(N_DP, -1).astype(jnp.int32)
    replica_counts = jnp.sum((per_replica[:, :, None] == expert_ids[None, None, :]).astype(jnp.int32), axis=1)
    slot_load = replica_counts[:, engine_place].astype(jnp.float32) / (TOK_DEV * TOP)
    return mixed_sum.astype(jnp.bfloat16), slot_load
```

```python
import functools

import jax
import jax.numpy as jnp
from jax import lax
from jax.experimental import pallas as pl
from jax.experimental.pallas import tpu as pltpu
from jax.sharding import PartitionSpec as P

MESH = pl.DeviceIdType.MESH
NX, NY, NZ = 4, 4, 16
ZLO = 8
D = 2048
FF = 768
HALF = FF // 2
ROWS = 16
TOP = 8
CAP = 4
PIECE = 128
COL = NZ * ROWS
SEND = NZ * CAP
CHUNKS = 2
WIDTH = D // CHUNKS
STEPS = NZ // 2
BF16, F32 = jnp.bfloat16, jnp.float32


def device(x, y, z, core):
    return (x * 2 + z // ZLO, (y * ZLO + z % ZLO) * 2 + core)


def layer_kernel(
    place_ref, engine_ref, weights, tokens_ref, routes_ref, gates_ref,
    mixed_ref, load_ref,
    matrix, token_all, meta_all, rows_out, rows_all, pick_hi, pick_lo, hidden,
    cross_out, cross_in, own_sum, back_out, back_in, mixing, ring_out, ring_in,
    hist_out, hist_in,
    local_sem, send_sem, matrix_sem, token_sem, meta_sem, rows_sem, twin_sem,
    cross_sem, back_sem, ring_sem, hist_sem,
):
    dp, ep = lax.axis_index("dp"), lax.axis_index("ep")
    x, z_hi = dp // 2, dp % 2
    y, z_lo, core = ep // 16, (ep // 2) % ZLO, ep % 2
    z = z_hi * ZLO + z_lo
    far = (z + ZLO) % NZ
    z_other = 1 - z_hi
    twin = 1 - core

    token_all[z] = tokens_ref[...]
    own_meta = jnp.zeros((ROWS, 128), F32)
    meta_all[z] = own_meta
    meta_all[z, :, 0:TOP] = routes_ref[...].astype(F32)
    meta_all[z, :, TOP:2 * TOP] = gates_ref[...]

    partners = []
    for k in range(NX):
        for other in (core, twin):
            if not (k == 0 and other is core):
                partners.append(device((x + k) % NX, y, z, other))
    for k in range(1, NY):
        for other in (core, twin):
            partners.append(device(x, (y + k) % NY, z, other))
    for other in (core, twin):
        partners.append(device(x, y, far, other))
    right = device(x, y, (z + 1) % NZ, core)
    left = device(x, y, (z + NZ - 1) % NZ, core)
    partners += [right, left]
    barrier = pltpu.get_barrier_semaphore()
    for partner in partners:
        pl.semaphore_signal(barrier, inc=1, device_id=partner, device_id_type=MESH)
    pl.semaphore_wait(barrier, len(partners))

    sends = []

    def send(src, dst, sem, to):
        copy = pltpu.make_async_remote_copy(
            src_ref=src, dst_ref=dst, send_sem=send_sem.at[len(sends)], recv_sem=sem,
            device_id=to, device_id_type=MESH,
        )
        copy.start()
        sends.append(copy)

    def arrived(ref, sem):
        pltpu.make_async_copy(ref, ref, sem).wait()

    def piece(part, core_of, dp_of):
        return matrix.at[part, pl.ds(pl.multiple_of(core_of * 1024 + dp_of * PIECE, PIECE), PIECE)]

    def own_piece(slot, part, half):
        return weights.at[slot, :, pl.ds(pl.multiple_of(part * FF + half * HALF, 128), HALF)]

    def piece_arrived(part, core_of, dp_of):
        arrived(piece(part, core_of, dp_of), matrix_sem.at[part, core_of * 8 + dp_of])

    def cross_part(part):
        for half in (core, twin):
            send(own_piece(z_other, part, half), piece(part, core, dp),
                 matrix_sem.at[part, core * 8 + dp], device(x, y, far, half))

    locals_ = []

    def spread_part(part):
        copy = pltpu.make_async_copy(own_piece(z_hi, part, core), piece(part, core, dp), local_sem.at[part])
        copy.start()
        locals_.append(copy)
        for half in (core, twin):
            for k in (1, 3, 2, 0):
                if k == 0 and half is core:
                    continue
                send(own_piece(z_hi, part, half), piece(part, core, dp),
                     matrix_sem.at[part, core * 8 + dp], device((x + k) % NX, y, z, half))

    def relay_part(part):
        dp_far = x * 2 + z_other
        for core_of in (core, twin):
            piece_arrived(part, core_of, dp_far)
            for k in (1, 3, 2):
                send(piece(part, core_of, dp_far), piece(part, core_of, dp_far),
                     matrix_sem.at[part, core_of * 8 + dp_far], device((x + k) % NX, y, z, core))

    def part_arrived(part):
        locals_[part].wait()
        for k in range(NX):
            for core_of in (core, twin):
                if not (k == 0 and core_of is core):
                    piece_arrived(part, core_of, ((x + k) % NX) * 2 + z_hi)
                if k > 0:
                    piece_arrived(part, core_of, ((x + k) % NX) * 2 + z_other)

    def token_view(block, step, way):
        if step == STEPS:
            return token_all.at[block, :, pl.ds(way * (D // 2), D // 2)]
        return token_all.at[block]

    def token_send(step):
        block = (z + NZ - step + 1) % NZ
        send(token_view(block, step, 0), token_view(block, step, 0), token_sem.at[0, step - 1], right)
        send(meta_all.at[block], meta_all.at[block], meta_sem.at[0, step - 1], right)
        block = (z + step - 1) % NZ
        send(token_view(block, step, 1), token_view(block, step, 1), token_sem.at[1, step - 1], left)
        if step < STEPS:
            send(meta_all.at[block], meta_all.at[block], meta_sem.at[1, step - 1], left)

    def token_arrived(step):
        block = (z + NZ - step) % NZ
        arrived(token_view(block, step, 0), token_sem.at[0, step - 1])
        arrived(meta_all.at[block], meta_sem.at[0, step - 1])
        block = (z + step) % NZ
        arrived(token_view(block, step, 1), token_sem.at[1, step - 1])
        if step < STEPS:
            arrived(meta_all.at[block], meta_sem.at[1, step - 1])

    token_send(1)
    for part in range(3):
        cross_part(part)
    for part in range(3):
        spread_part(part)
    for step in range(1, STEPS + 1):
        token_arrived(step)
        if step < STEPS:
            token_send(step + 1)
        if step == STEPS // 2:
            relay_part(0)

    turned = meta_all[...].reshape(COL, 128).T
    chosen, gate = turned[0:TOP], turned[TOP:2 * TOP]
    expert_row = lax.broadcasted_iota(jnp.int32, (64, COL), 0).astype(F32)
    lane64 = lax.broadcasted_iota(jnp.int32, (64, COL), 1)
    named = jnp.zeros((64, COL), F32)
    for k in range(TOP):
        named = named + jnp.where(chosen[k:k + 1] == expert_row, 1.0, 0.0)
    ours = jnp.where(
        lax.broadcasted_iota(jnp.int32, (8, COL), 1) // (COL // 2) == z_hi, 1.0, 0.0)
    hist_out[...] = lax.dot_general(
        ours, jnp.concatenate([named, jnp.zeros((64, COL), F32)], axis=0),
        (((1,), (1,)), ((), ())), preferred_element_type=F32)
    hist_in[0] = hist_out[...]
    for k in range(NY):
        for index, other in enumerate((core, twin)):
            if k + index > 0:
                send(hist_out, hist_in.at[2 * k + index], hist_sem.at[2 * k + index],
                     device(x, (y + k) % NY, z, other))

    row8 = lax.broadcasted_iota(jnp.int32, (8, COL), 0)
    match = jnp.zeros((8, COL), F32)
    hits, weight = [], []
    for k in range(NY):
        wanted = place_ref[2 * (((y + k) % NY) * ZLO + z_lo) + z_hi].astype(F32)
        same = jnp.where(chosen == wanted, 1.0, 0.0)
        hits.append(jnp.sum(same, axis=0, keepdims=True))
        weight.append(jnp.sum(same * gate, axis=0, keepdims=True))
        match = match + jnp.where(row8 == k, hits[k], 0.0)
    before = lax.broadcasted_iota(jnp.int32, (COL, COL), 0)
    after = lax.broadcasted_iota(jnp.int32, (COL, COL), 1)
    earlier = jnp.where((before < after) & (before // ROWS == after // ROWS), 1.0, 0.0).astype(BF16)
    rank = jnp.dot(match.astype(BF16), earlier, preferred_element_type=F32)
    sent_row = lax.broadcasted_iota(jnp.int32, (SEND, COL), 0)
    sent_rank = (sent_row % CAP).astype(F32)
    same_block = sent_row // CAP == lane64 // ROWS
    picks = []
    for k in range(NY):
        picks.append(jnp.where(same_block & (sent_rank == rank[k:k + 1]), hits[k], 0.0))
    pick = jnp.concatenate(picks, axis=0)
    scaled = jnp.concatenate([picks[k] * weight[k] for k in range(NY)], axis=0).T
    high = scaled.astype(BF16)
    pick_hi[...] = high
    pick_lo[...] = (scaled - high.astype(F32)).astype(BF16)
    pick = pick.astype(BF16)
    every = token_all[...].reshape(COL, D)
    for k in (2, 1, 3, 0):
        moved = jnp.dot(pick[k * SEND:(k + 1) * SEND], every, preferred_element_type=F32).astype(BF16)
        if k == 0:
            rows_all[core, y] = moved
            send(rows_all.at[core, y], rows_all.at[core, y], twin_sem.at[0], device(x, y, z, twin))
        else:
            rows_out[k - 1] = moved
            send(rows_out.at[k - 1], rows_all.at[core, y], rows_sem.at[k], device(x, (y + k) % NY, z, core))
    relay_part(1)
    for k in (1, 3, 2):
        giver = (y + NY - k) % NY
        arrived(rows_all.at[core, giver], rows_sem.at[k])
        send(rows_all.at[core, giver], rows_all.at[core, giver], twin_sem.at[k], device(x, y, z, twin))
    for k in range(NY):
        arrived(rows_all.at[twin, (y + NY - k) % NY], twin_sem.at[k])

    part_arrived(0)
    part_arrived(1)
    for plane in range(2):
        rows = rows_all[plane].reshape(NY * SEND, D)
        a = jnp.dot(rows, matrix[0], preferred_element_type=F32)
        b = jnp.dot(rows, matrix[1], preferred_element_type=F32)
        hidden[plane] = (a / (1.0 + jnp.exp(-a)) * b).astype(BF16)
    relay_part(2)
    part_arrived(2)

    def cols(chunk):
        return pl.ds(chunk * WIDTH, WIDTH)

    nt = (((1,), (1,)), ((), ()))
    for chunk in range(CHUNKS):
        down = matrix[2, cols(chunk)]
        cross_out[chunk] = lax.dot_general(hidden[twin], down, nt, preferred_element_type=F32).astype(BF16)
        send(cross_out.at[chunk], cross_in.at[chunk], cross_sem.at[chunk], device(x, y, z, twin))
    for chunk in range(CHUNKS):
        down = matrix[2, cols(chunk)]
        own_sum[chunk] = lax.dot_general(hidden[core], down, nt, preferred_element_type=F32)
    for chunk in range(CHUNKS):
        arrived(cross_in.at[chunk], cross_sem.at[chunk])
        total = (own_sum[chunk] + cross_in[chunk].astype(F32)).astype(BF16)
        back_out[chunk] = total.reshape(NY, SEND, WIDTH)
        for k in (2, 1, 3):
            giver = (y + NY - k) % NY
            send(back_out.at[chunk, giver], back_in.at[chunk, k], back_sem.at[chunk, k], device(x, giver, z, core))
        back_in[chunk, 0] = back_out[chunk, y]

    def ring_send(step, chunk):
        send(ring_out.at[0, step - 1, chunk], ring_in.at[0, step - 1, chunk], ring_sem.at[0, step - 1, chunk], right)
        if step < STEPS:
            send(ring_out.at[1, step - 1, chunk], ring_in.at[1, step - 1, chunk], ring_sem.at[1, step - 1, chunk], left)

    for chunk in range(CHUNKS):
        for k in (1, 3, 2):
            arrived(back_in.at[chunk, k], back_sem.at[chunk, k])
        got = back_in[chunk].reshape(NY * SEND, WIDTH)
        total = jnp.dot(pick_hi[...], got, preferred_element_type=F32)
        total = total + jnp.dot(pick_lo[...], got, preferred_element_type=F32)
        mixing[chunk] = total.reshape(NZ, ROWS, WIDTH)
        ring_out[0, 0, chunk] = mixing[chunk, (z + STEPS) % NZ].astype(BF16)
        ring_out[1, 0, chunk] = mixing[chunk, (z + NZ - STEPS + 1) % NZ].astype(BF16)
        ring_send(1, chunk)
    for step in range(1, STEPS):
        for chunk in range(CHUNKS):
            arrived(ring_in.at[0, step - 1, chunk], ring_sem.at[0, step - 1, chunk])
            block = mixing[chunk, (z + STEPS - step) % NZ] + ring_in[0, step - 1, chunk].astype(F32)
            ring_out[0, step, chunk] = block.astype(BF16)
            if step < STEPS - 1:
                arrived(ring_in.at[1, step - 1, chunk], ring_sem.at[1, step - 1, chunk])
                block = mixing[chunk, (z + NZ - STEPS + 1 + step) % NZ] + ring_in[1, step - 1, chunk].astype(F32)
                ring_out[1, step, chunk] = block.astype(BF16)
            if step < STEPS - 1:
                ring_send(step + 1, chunk)
            else:
                send(ring_out.at[0, step, chunk], ring_in.at[0, step, chunk], ring_sem.at[0, step, chunk], right)
    for chunk in range(CHUNKS):
        arrived(ring_in.at[1, STEPS - 2, chunk], ring_sem.at[1, STEPS - 2, chunk])
        arrived(ring_in.at[0, STEPS - 1, chunk], ring_sem.at[0, STEPS - 1, chunk])
        block = mixing[chunk, z] + ring_in[0, STEPS - 1, chunk].astype(F32) + ring_in[1, STEPS - 2, chunk].astype(F32)
        mixed_ref[:, cols(chunk)] = block.astype(BF16)

    for index in range(1, 2 * NY):
        arrived(hist_in.at[index], hist_sem.at[index])
    counts = jnp.sum(hist_in[...], axis=0)
    lane = lax.broadcasted_iota(jnp.int32, (8, 128), 1)
    mine = jnp.sum(jnp.where(lane == engine_ref[ep], counts, 0.0), axis=1, keepdims=True)
    load_ref[...] = mine[0:1] / (ROWS * TOP)
    for copy in sends:
        copy.wait_send()


def on_device(trainer_weights, trainer_place, engine_place, tokens, routes, gates):
    smem = pl.BlockSpec(memory_space=pltpu.SMEM)
    vmem = pl.BlockSpec(memory_space=pltpu.VMEM)
    dma = pltpu.SemaphoreType.DMA
    return pl.pallas_call(
        layer_kernel,
        out_shape=(
            jax.ShapeDtypeStruct((ROWS, D), BF16),
            jax.ShapeDtypeStruct((1, 1), F32),
        ),
        in_specs=[smem, smem, pl.BlockSpec(memory_space=pl.ANY), vmem, vmem, vmem],
        out_specs=(vmem, vmem),
        scratch_shapes=[
            pltpu.VMEM((3, D, HALF), BF16),
            pltpu.VMEM((NZ, ROWS, D), BF16),
            pltpu.VMEM((NZ, ROWS, 128), F32),
            pltpu.VMEM((NY - 1, SEND, D), BF16),
            pltpu.VMEM((2, NY, SEND, D), BF16),
            pltpu.VMEM((COL, NY * SEND), BF16),
            pltpu.VMEM((COL, NY * SEND), BF16),
            pltpu.VMEM((2, NY * SEND, HALF), BF16),
            pltpu.VMEM((CHUNKS, NY * SEND, WIDTH), BF16),
            pltpu.VMEM((CHUNKS, NY * SEND, WIDTH), BF16),
            pltpu.VMEM((CHUNKS, NY * SEND, WIDTH), F32),
            pltpu.VMEM((CHUNKS, NY, SEND, WIDTH), BF16),
            pltpu.VMEM((CHUNKS, NY, SEND, WIDTH), BF16),
            pltpu.VMEM((CHUNKS, NZ, ROWS, WIDTH), F32),
            pltpu.VMEM((2, STEPS, CHUNKS, ROWS, WIDTH), BF16),
            pltpu.VMEM((2, STEPS, CHUNKS, ROWS, WIDTH), BF16),
            pltpu.VMEM((8, 128), F32),
            pltpu.VMEM((2 * NY, 8, 128), F32),
            dma((3,)),
            dma((160,)),
            dma((3, 16)),
            dma((2, STEPS)),
            dma((2, STEPS)),
            dma((NY,)),
            dma((NY,)),
            dma((CHUNKS,)),
            dma((CHUNKS, NY)),
            dma((2, STEPS, CHUNKS)),
            dma((2 * NY,)),
        ],
        compiler_params=pltpu.CompilerParams(
            collective_id=0, has_side_effects=True, vmem_limit_bytes=48 * 2**20
        ),
    )(trainer_place, engine_place, trainer_weights[0], tokens, routes, gates)


def solution(mesh):
    in_specs = (
        P("ep", None, "dp", None),
        P(),
        P(),
        P(("dp", "ep"), None),
        P(("dp", "ep"), None),
        P(("dp", "ep"), None),
    )
    out_specs = (P(("dp", "ep"), None), P("dp", "ep"))
    return jax.shard_map(
        on_device, mesh=mesh, in_specs=in_specs, out_specs=out_specs, check_vma=False
    )
```

```python
import functools

import jax
import jax.numpy as jnp
from jax import lax
from jax.experimental import pallas as pl
from jax.experimental.pallas import tpu as pltpu
from jax.sharding import PartitionSpec as P

MESH = pl.DeviceIdType.MESH
NX, NY, NZ = 4, 4, 16
ZLO = 8
D = 2048
FF = 768
HALF = FF // 2
ROWS = 16
TOP = 8
CAP = 4
PIECE = 128
COL = NZ * ROWS
SEND = NZ * CAP
CHUNKS = 4
WIDTH = D // CHUNKS
PART = PIECE // CHUNKS
STEPS = NZ // 2
BF16, F32 = jnp.bfloat16, jnp.float32
META = 128
ORDER = (
    "t0", "c0", "s0", "s1", "s2", "t1", "t2", "c1", "t3", "r0", "t4",
    "C0", "C1", "d", "r1", "C2", "C3", "w", "h", "a",
)
STRIDE = 2


def device(x, y, z, core):
    return (x * 2 + z // ZLO, (y * ZLO + z % ZLO) * 2 + core)


def layer_kernel(
    place_any, engine_any, weights, tokens_ref, routes_any, gates_any,
    mixed_ref, load_ref,
    matrix, down_all, token_all, rows_out, rows_all, pick_hi, pick_lo, hidden,
    cross_out, cross_in, own_sum, back_out, back_in, mixing, ring_out, ring_in, final,
    hist_out, hist_in, place_ref, engine_ref, routes_ref, gates_ref,
    local_sem, send_sem, matrix_sem, token_sem, rows_sem, twin_sem,
    cross_sem, back_sem, ring_sem, hist_sem,
):
    dp, ep = lax.axis_index("dp"), lax.axis_index("ep")
    x, z_hi = dp // 2, dp % 2
    y, z_lo, core = ep // 16, (ep // 2) % ZLO, ep % 2
    z = z_hi * ZLO + z_lo
    far = (z + ZLO) % NZ
    z_other = 1 - z_hi
    twin = 1 - core

    fetches = [
        pltpu.make_async_copy(src, dst, local_sem.at[3 + index])
        for index, (src, dst) in enumerate((
            (routes_any, routes_ref), (gates_any, gates_ref), (tokens_ref, token_all.at[z, :, pl.ds(0, D)]),
            (place_any, place_ref), (engine_any, engine_ref)))
    ]
    for copy in fetches:
        copy.start()
    partners = []
    for k in range(NX):
        for other in (core, twin):
            if not (k == 0 and other is core):
                partners.append(device((x + k) % NX, y, z, other))
    for k in range(1, NY):
        for other in (core, twin):
            partners.append(device(x, (y + k) % NY, z, other))
    for other in (core, twin):
        partners.append(device(x, y, far, other))
    along = {step: device(x, y, (z + NZ + step) % NZ, core) for step in (1, 2, -1, -2)}
    partners += list(along.values())
    barrier = pltpu.get_barrier_semaphore()
    for partner in partners:
        pl.semaphore_signal(barrier, inc=1, device_id=partner, device_id_type=MESH)
    for copy in fetches:
        copy.wait()
    gate_parts, rest = [], gates_ref[...]
    for _ in range(3):
        gate_parts.append(rest.astype(BF16).astype(F32))
        rest = rest - gate_parts[-1]
    facts = jnp.concatenate([routes_ref[...].astype(F32)] + gate_parts, axis=0)
    facts = jnp.concatenate([facts, jnp.zeros((4 * TOP, META - ROWS), F32)], axis=1)
    facts = jnp.concatenate([facts, jnp.zeros((META - 4 * TOP, META), F32)], axis=0)
    token_all[z, :, D:] = facts.T[0:ROWS].astype(BF16)
    pl.semaphore_wait(barrier, len(partners))

    sends, waited = [], []

    def send(src, dst, sem, to):
        copy = pltpu.make_async_remote_copy(
            src_ref=src, dst_ref=dst, send_sem=send_sem.at[len(sends)], recv_sem=sem,
            device_id=to, device_id_type=MESH,
        )
        copy.start()
        sends.append(copy)
        return copy

    def arrived(ref, sem):
        pltpu.make_async_copy(ref, ref, sem).wait()

    def piece(part, core_of, dp_of, first=0, count=CHUNKS):
        source = core_of * 8 + dp_of
        if part < 2:
            return matrix.at[part, source, pl.ds(first, count)]
        return down_all.at[pl.ds(first, count), source]

    def piece_sem(part, core_of, dp_of, first=0, count=CHUNKS):
        return matrix_sem.at[part, core_of * 8 + dp_of, first]

    def own_piece(slot, part, half, first=0, count=CHUNKS):
        columns = pl.ds(pl.multiple_of(part * FF + half * HALF, 128), HALF)
        return weights.at[slot, pl.ds(first, count), :, columns]

    def piece_arrived(*at):
        arrived(piece(*at), piece_sem(*at))

    crossing = {}

    def crossed(part, *chunks):
        for copy in crossing.pop((part,) + chunks):
            copy.wait_send()
            waited.append(copy)

    def cross_part(part, *chunks):
        crossing[(part,) + chunks] = []
        for half in (core, twin):
            crossing[(part,) + chunks].append(send(own_piece(z_other, part, half, *chunks), piece(part, core, dp, *chunks),
                 piece_sem(part, core, dp, *chunks), device(x, y, far, half)))

    locals_ = {}

    def spread_part(part):
        locals_[part] = pltpu.make_async_copy(
            own_piece(z_hi, part, core), piece(part, core, dp), local_sem.at[part])
        locals_[part].start()
        for half in (core, twin):
            for k in (1, 3, 2, 0):
                if k == 0 and half is core:
                    continue
                send(own_piece(z_hi, part, half), piece(part, core, dp),
                     piece_sem(part, core, dp), device((x + k) % NX, y, z, half))

    relayed = {0: [], 1: [], 2: []}

    def relay_part(part, *chunks):
        dp_far = x * 2 + z_other
        relayed[part].append(chunks)
        for core_of in (core, twin):
            piece_arrived(part, core_of, dp_far, *chunks)
            for k in (2, 1, 3):
                send(piece(part, core_of, dp_far, *chunks), piece(part, core_of, dp_far, *chunks),
                     piece_sem(part, core_of, dp_far, *chunks), device((x + k) % NX, y, z, core))

    def spread_arrived(part):
        locals_[part].wait()
        for k in range(NX):
            for core_of in (core, twin):
                if not (k == 0 and core_of is core):
                    piece_arrived(part, core_of, ((x + k) % NX) * 2 + z_hi)

    def relay_arrived(part, *chunks):
        for k in range(1, NX):
            for core_of in (core, twin):
                piece_arrived(part, core_of, ((x + k) % NX) * 2 + z_other, *chunks)

    def token_view(block, distance, way):
        if distance == STEPS:
            return token_all.at[block, :, pl.ds((1 - way) * (D // 2), D // 2 + (1 - way) * META)]
        return token_all.at[block]

    def token_send(group, way):
        sign = 1 - 2 * way
        block = (z + NZ - sign * STRIDE * group) % NZ
        for hop in range(STRIDE, 0, -1):
            distance = STRIDE * group + hop
            send(token_view(block, distance, way), token_view(block, distance, way),
                 token_sem.at[way, distance - 1], along[sign * hop])

    def token_group(group):
        for way in range(2):
            if group == 0:
                token_send(0, way)
                continue
            sign = 1 - 2 * way
            block = (z + NZ - sign * STRIDE * group) % NZ
            arrived(token_view(block, STRIDE * group, way), token_sem.at[way, STRIDE * group - 1])
            if group < STEPS // STRIDE:
                token_send(group, way)
        if group == STEPS // STRIDE:
            for way in range(2):
                for distance in [at for at in range(1, STEPS) if at % STRIDE]:
                    block = (z + NZ - (1 - 2 * way) * distance) % NZ
                    arrived(token_view(block, distance, way), token_sem.at[way, distance - 1])

    def dispatch():
        turned = token_all[:, :, D:].reshape(COL, META).astype(F32).T
        chosen = turned[0:TOP]
        gate = turned[TOP:2 * TOP] + turned[2 * TOP:3 * TOP] + turned[3 * TOP:4 * TOP]
        lane64 = lax.broadcasted_iota(jnp.int32, (64, COL), 1)
        row8 = lax.broadcasted_iota(jnp.int32, (8, COL), 0)
        match = jnp.zeros((8, COL), F32)
        hits, weight = [], []
        for k in range(NY):
            wanted = place_ref[2 * (((y + k) % NY) * ZLO + z_lo) + z_hi].astype(F32)
            same = jnp.where(chosen == wanted, 1.0, 0.0)
            hits.append(jnp.sum(same, axis=0, keepdims=True))
            weight.append(jnp.sum(same * gate, axis=0, keepdims=True))
            match = match + jnp.where(row8 == k, hits[k], 0.0)
        before = lax.broadcasted_iota(jnp.int32, (COL, COL), 0)
        after = lax.broadcasted_iota(jnp.int32, (COL, COL), 1)
        earlier = jnp.where((before < after) & (before // ROWS == after // ROWS), 1.0, 0.0).astype(BF16)
        rank = jnp.dot(match.astype(BF16), earlier, preferred_element_type=F32)
        sent_row = lax.broadcasted_iota(jnp.int32, (SEND, COL), 0)
        sent_rank = (sent_row % CAP).astype(F32)
        same_block = sent_row // CAP == lane64 // ROWS
        picks = []
        for k in range(NY):
            picks.append(jnp.where(same_block & (sent_rank == rank[k:k + 1]), hits[k], 0.0))
        pick = jnp.concatenate(picks, axis=0)
        scaled = jnp.concatenate([picks[k] * weight[k] for k in range(NY)], axis=0).T
        high = scaled.astype(BF16)
        pick_hi[...] = high
        pick_lo[...] = (scaled - high.astype(F32)).astype(BF16)
        pick = pick.astype(BF16)
        every = token_all[:, :, 0:D].reshape(COL, D)
        for k in (2, 1, 3, 0):
            moved = jnp.dot(pick[k * SEND:(k + 1) * SEND], every, preferred_element_type=F32).astype(BF16)
            if k == 0:
                rows_all[core, y] = moved
                send(rows_all.at[core, y], rows_all.at[core, y], twin_sem.at[0], device(x, y, z, twin))
            else:
                rows_out[k - 1] = moved
                send(rows_out.at[k - 1], rows_all.at[core, y], rows_sem.at[k], device(x, (y + k) % NY, z, core))

    def count():
        chosen = token_all[:, :, D:].reshape(COL, META).astype(F32).T[0:TOP]
        expert_row = lax.broadcasted_iota(jnp.int32, (64, COL), 0).astype(F32)
        named = jnp.zeros((64, COL), F32)
        for k in range(TOP):
            named = named + jnp.where(chosen[k:k + 1] == expert_row, 1.0, 0.0)
        ours = jnp.where(
            lax.broadcasted_iota(jnp.int32, (8, COL), 1) // (COL // 2) == z_hi, 1.0, 0.0)
        hist_out[...] = lax.dot_general(
            ours, jnp.concatenate([named, jnp.zeros((64, COL), F32)], axis=0),
            (((1,), (1,)), ((), ())), preferred_element_type=F32)
        hist_in[0] = hist_out[...]
        for k in range(NY):
            for index, other in enumerate((core, twin)):
                if k + index > 0:
                    send(hist_out, hist_in.at[2 * k + index], hist_sem.at[2 * k + index],
                         device(x, (y + k) % NY, z, other))

    def exchange_rows():
        for k in (1, 3, 2):
            giver = (y + NY - k) % NY
            arrived(rows_all.at[core, giver], rows_sem.at[k])
            send(rows_all.at[core, giver], rows_all.at[core, giver], twin_sem.at[k], device(x, y, z, twin))
        for k in range(NY):
            arrived(rows_all.at[twin, (y + NY - k) % NY], twin_sem.at[k])

    def first_products():
        for part in range(2):
            spread_arrived(part)
            for chunks in relayed[part]:
                relay_arrived(part, *chunks)
        for plane in range(2):
            rows = rows_all[plane].reshape(NY * SEND, D)
            a = jnp.dot(rows, matrix[0].reshape(D, HALF), preferred_element_type=F32)
            b = jnp.dot(rows, matrix[1].reshape(D, HALF), preferred_element_type=F32)
            hidden[plane] = (a / (1.0 + jnp.exp(-a)) * b).astype(BF16)

    nt = (((1,), (1,)), ((), ()))

    def down_products(chunk):
        if chunk == 0:
            spread_arrived(2)
        relay_arrived(2, chunk, 1)
        down = down_all[chunk].reshape(WIDTH, HALF)
        cross_out[chunk] = lax.dot_general(hidden[twin], down, nt, preferred_element_type=F32).astype(BF16)
        send(cross_out.at[chunk], cross_in.at[chunk], cross_sem.at[chunk], device(x, y, z, twin))
        own_sum[chunk] = lax.dot_general(hidden[core], down, nt, preferred_element_type=F32)

    def rows_back(chunk):
        arrived(cross_in.at[chunk], cross_sem.at[chunk])
        total = (own_sum[chunk] + cross_in[chunk].astype(F32)).astype(BF16)
        back_out[chunk] = total.reshape(NY, SEND, WIDTH)
        for k in (2, 1, 3):
            giver = (y + NY - k) % NY
            send(back_out.at[chunk, giver], back_in.at[chunk, k], back_sem.at[chunk, k], device(x, giver, z, core))
        back_in[chunk, 0] = back_out[chunk, y]

    def reach(chunk, way):
        return STEPS if chunk % 2 == way else STEPS - 2

    def block_of(way, distance):
        return (z + NZ + (1 - 2 * way) * distance) % NZ

    def ring_send(chunk, way, distance):
        hop = 2 - distance % 2
        send(ring_out.at[way, distance - 1, chunk], ring_in.at[way, distance - 1, chunk],
             ring_sem.at[way, distance - 1, chunk], along[(1 - 2 * way) * hop])

    def ring_sum(chunk, way, distance):
        total = mixing[chunk, block_of(way, distance)] if distance else 0.0
        for farther in (distance + 1, distance + 2):
            if farther <= max(reach(chunk, way), STEPS - 1):
                arrived(ring_in.at[way, farther - 1, chunk], ring_sem.at[way, farther - 1, chunk])
                total = total + ring_in[way, farther - 1, chunk].astype(F32)
        return total

    def mix(chunk):
        for k in (1, 3, 2):
            arrived(back_in.at[chunk, k], back_sem.at[chunk, k])
        got = back_in[chunk].reshape(NY * SEND, WIDTH)
        total = jnp.dot(pick_hi[...], got, preferred_element_type=F32)
        total = total + jnp.dot(pick_lo[...], got, preferred_element_type=F32)
        mixing[chunk] = total.reshape(NZ, ROWS, WIDTH)
        for distance in (8, 7, 5, 3, 1):
            for way in range(2):
                if distance <= reach(chunk, way) or distance % 2:
                    ring_out[way, distance - 1, chunk] = mixing[chunk, block_of(way, distance)].astype(BF16)
                    ring_send(chunk, way, distance)

    def ring_step(chunk, distance):
        for way in (chunk % 2, 1 - chunk % 2):
            ring_out[way, distance - 1, chunk] = ring_sum(chunk, way, distance).astype(BF16)
            ring_send(chunk, way, distance)

    def finish(chunk):
        total = mixing[chunk, z] + ring_sum(chunk, 0, 0) + ring_sum(chunk, 1, 0)
        lane = lax.broadcasted_iota(jnp.int32, (ROWS, PIECE), 1)
        for p in range(D // PIECE):
            first = p // CHUNKS * PIECE
            moved = total[:, first:first + PIECE]
            shift = (chunk - p % CHUNKS) % CHUNKS * PART
            if shift:
                moved = pltpu.roll(moved, shift, 1)
            at = pl.ds(p * PIECE, PIECE)
            if chunk == 0:
                final[:, at] = moved
            elif chunk < CHUNKS - 1:
                final[:, at] = jnp.where(lane // PART == chunk, moved, final[:, at])
            else:
                mixed_ref[:, at] = jnp.where(lane // PART == chunk, moved, final[:, at]).astype(BF16)

    stages = {
        "p": crossed, "d": dispatch, "w": exchange_rows, "a": first_products, "h": count,
        "t": token_group, "c": cross_part, "s": spread_part, "r": relay_part,
        "C": lambda chunk: cross_part(2, chunk, 1), "R": lambda chunk: relay_part(2, chunk, 1),
        "Y": down_products, "b": rows_back, "m": mix, "f": finish,
        "x": lambda chunk: ring_step(chunk, 6), "y": lambda chunk: ring_step(chunk, 4),
        "z": lambda chunk: ring_step(chunk, 2),
    }
    for event in ORDER:
        stages[event[0]](*[int(digit) for digit in event[1:]])
    for slot in range(CHUNKS + 7):
        for late, name in enumerate("RYbmxyzf"):
            if 0 <= slot - late < CHUNKS and name + str(slot - late) not in ORDER:
                stages[name](slot - late)

    for index in range(1, 2 * NY):
        arrived(hist_in.at[index], hist_sem.at[index])
    counts = jnp.sum(hist_in[...], axis=0)
    lane = lax.broadcasted_iota(jnp.int32, (8, 128), 1)
    mine = jnp.sum(jnp.where(lane == engine_ref[ep], counts, 0.0), axis=1, keepdims=True)
    load_ref[...] = mine[0:1] / (ROWS * TOP)
    for copy in sends:
        if not any(copy is other for other in waited):
            copy.wait_send()


def on_device(trainer_weights, trainer_place, engine_place, tokens, routes, gates):
    vmem = pl.BlockSpec(memory_space=pltpu.VMEM)
    dma = pltpu.SemaphoreType.DMA
    return pl.pallas_call(
        layer_kernel,
        out_shape=(
            jax.ShapeDtypeStruct((ROWS, D), BF16),
            jax.ShapeDtypeStruct((1, 1), F32),
        ),
        in_specs=[pl.BlockSpec(memory_space=pl.ANY)] * 6,
        out_specs=(vmem, vmem),
        scratch_shapes=[
            pltpu.VMEM((2, 16, CHUNKS, PART, HALF), BF16),
            pltpu.VMEM((CHUNKS, 16, PART, HALF), BF16),
            pltpu.VMEM((NZ, ROWS, D + META), BF16),
            pltpu.VMEM((NY - 1, SEND, D), BF16),
            pltpu.VMEM((2, NY, SEND, D), BF16),
            pltpu.VMEM((COL, NY * SEND), BF16),
            pltpu.VMEM((COL, NY * SEND), BF16),
            pltpu.VMEM((2, NY * SEND, HALF), BF16),
            pltpu.VMEM((CHUNKS, NY * SEND, WIDTH), BF16),
            pltpu.VMEM((CHUNKS, NY * SEND, WIDTH), BF16),
            pltpu.VMEM((CHUNKS, NY * SEND, WIDTH), F32),
            pltpu.VMEM((CHUNKS, NY, SEND, WIDTH), BF16),
            pltpu.VMEM((CHUNKS, NY, SEND, WIDTH), BF16),
            pltpu.VMEM((CHUNKS, NZ, ROWS, WIDTH), F32),
            pltpu.VMEM((2, STEPS, CHUNKS, ROWS, WIDTH), BF16),
            pltpu.VMEM((2, STEPS, CHUNKS, ROWS, WIDTH), BF16),
            pltpu.VMEM((ROWS, D), F32),
            pltpu.VMEM((8, 128), F32),
            pltpu.VMEM((2 * NY, 8, 128), F32),
            pltpu.SMEM((NZ * NY,), jnp.int32),
            pltpu.SMEM((NZ * NY,), jnp.int32),
            pltpu.VMEM((TOP, ROWS), jnp.int32),
            pltpu.VMEM((TOP, ROWS), F32),
            dma((8,)),
            dma((192,)),
            dma((3, 16, CHUNKS)),
            dma((2, STEPS)),
            dma((NY,)),
            dma((NY,)),
            dma((CHUNKS,)),
            dma((CHUNKS, NY)),
            dma((2, STEPS, CHUNKS)),
            dma((2 * NY,)),
        ],
        compiler_params=pltpu.CompilerParams(
            collective_id=0, has_side_effects=True, vmem_limit_bytes=60 * 2**20
        ),
    )(trainer_place, engine_place, trainer_weights[0].reshape(2, CHUNKS, PART, 3 * FF), tokens, routes.T, gates.T)


def solution(mesh):
    in_specs = (
        P("ep", None, "dp", None),
        P(),
        P(),
        P(("dp", "ep"), None),
        P(("dp", "ep"), None),
        P(("dp", "ep"), None),
    )
    out_specs = (P(("dp", "ep"), None), P("dp", "ep"))
    return jax.shard_map(
        on_device, mesh=mesh, in_specs=in_specs, out_specs=out_specs, check_vma=False
    )
```

```python
import functools

import jax
import jax.numpy as jnp
from jax import lax
from jax.experimental import pallas as pl
from jax.experimental.pallas import tpu as pltpu
from jax.sharding import PartitionSpec as P

MESH = pl.DeviceIdType.MESH
NX, NY, NZ = 4, 4, 16
ZLO = 8
D = 2048
FF = 768
HALF = FF // 2
ROWS = 16
TOP = 8
CAP = 4
PIECE = 128
COL = NZ * ROWS
SEND = NZ * CAP
CHUNKS = 4
WIDTH = D // CHUNKS
PART = PIECE // CHUNKS
STEPS = NZ // 2
BF16, F32 = jnp.bfloat16, jnp.float32
META = 128
ORDER = (
    "t0", "c0", "s0", "s1", "s2", "t1", "t2", "c1", "t3", "r0", "t4",
    "d", "r1", "C0", "C1", "C2", "C3", "w", "h", "a",
)
STRIDE = 2
STOPS = ((6, 4, 2, 0), (6, 4, 2, 0), (6, 4, 2, 0), (5, 2, 0))


def device(x, y, z, core):
    return (x * 2 + z // ZLO, (y * ZLO + z % ZLO) * 2 + core)


def layer_kernel(
    place_any, engine_any, weights, tokens_ref, routes_any, gates_any,
    mixed_ref, load_ref,
    matrix, down_all, token_all, rows_out, rows_all, pick_hi, pick_lo, hidden,
    cross_out, cross_in, own_sum, back_out, back_in, mixing, ring_out, ring_in, final,
    hist_out, hist_in, place_ref, engine_ref, routes_ref, gates_ref,
    local_sem, send_sem, matrix_sem, token_sem, rows_sem, twin_sem,
    cross_sem, back_sem, ring_sem, hist_sem,
):
    dp, ep = lax.axis_index("dp"), lax.axis_index("ep")
    x, z_hi = dp // 2, dp % 2
    y, z_lo, core = ep // 16, (ep // 2) % ZLO, ep % 2
    z = z_hi * ZLO + z_lo
    far = (z + ZLO) % NZ
    z_other = 1 - z_hi
    twin = 1 - core

    fetches = [
        pltpu.make_async_copy(src, dst, local_sem.at[3 + index])
        for index, (src, dst) in enumerate((
            (routes_any, routes_ref), (gates_any, gates_ref), (tokens_ref, token_all.at[z, :, pl.ds(0, D)]),
            (place_any, place_ref), (engine_any, engine_ref)))
    ]
    for copy in fetches:
        copy.start()
    partners = [device(x, y, far, other) for other in (core, twin)]
    for k in range(NX):
        for other in (core, twin):
            if not (k == 0 and other is core):
                partners.append(device((x + k) % NX, y, z, other))
    for k in range(1, NY):
        for other in (core, twin):
            partners.append(device(x, (y + k) % NY, z, other))
    along = {step: device(x, y, (z + NZ + step) % NZ, core) for step in (1, 2, 3, -1, -2, -3)}
    partners += list(along.values())
    barrier = pltpu.get_barrier_semaphore()
    for partner in partners:
        pl.semaphore_signal(barrier, inc=1, device_id=partner, device_id_type=MESH)
    for copy in fetches:
        copy.wait()
    gate_parts, rest = [], gates_ref[...]
    for _ in range(3):
        gate_parts.append(rest.astype(BF16).astype(F32))
        rest = rest - gate_parts[-1]
    facts = jnp.concatenate([routes_ref[...].astype(F32)] + gate_parts, axis=0)
    facts = jnp.concatenate([facts, jnp.zeros((4 * TOP, META - ROWS), F32)], axis=1)
    facts = jnp.concatenate([facts, jnp.zeros((META - 4 * TOP, META), F32)], axis=0)
    token_all[z, :, D:] = facts.T[0:ROWS].astype(BF16)
    pl.semaphore_wait(barrier, len(partners))

    sends, waited = [], []

    def send(src, dst, sem, to):
        copy = pltpu.make_async_remote_copy(
            src_ref=src, dst_ref=dst, send_sem=send_sem.at[len(sends)], recv_sem=sem,
            device_id=to, device_id_type=MESH,
        )
        copy.start()
        sends.append(copy)
        return copy

    def arrived(ref, sem):
        pltpu.make_async_copy(ref, ref, sem).wait()

    def piece(part, core_of, dp_of, first=0, count=CHUNKS):
        source = core_of * 8 + dp_of
        if part < 2:
            return matrix.at[part, source, pl.ds(first, count)]
        return down_all.at[pl.ds(first, count), source]

    def piece_sem(part, core_of, dp_of, first=0, count=CHUNKS):
        return matrix_sem.at[part, core_of * 8 + dp_of, first]

    def own_piece(slot, part, half, first=0, count=CHUNKS):
        columns = pl.ds(pl.multiple_of(part * FF + half * HALF, 128), HALF)
        return weights.at[slot, pl.ds(first, count), :, columns]

    def piece_arrived(*at):
        arrived(piece(*at), piece_sem(*at))

    crossing = {}

    def crossed(part, *chunks):
        for copy in crossing.pop((part,) + chunks):
            copy.wait_send()
            waited.append(copy)

    def cross_part(part, *chunks):
        crossing[(part,) + chunks] = []
        for half in (core, twin):
            crossing[(part,) + chunks].append(send(own_piece(z_other, part, half, *chunks), piece(part, core, dp, *chunks),
                 piece_sem(part, core, dp, *chunks), device(x, y, far, half)))

    locals_ = {}

    def spread_part(part):
        locals_[part] = pltpu.make_async_copy(
            own_piece(z_hi, part, core), piece(part, core, dp), local_sem.at[part])
        locals_[part].start()
        for half in (core, twin):
            for k in (1, 3, 2, 0):
                if k == 0 and half is core:
                    continue
                send(own_piece(z_hi, part, half), piece(part, core, dp),
                     piece_sem(part, core, dp), device((x + k) % NX, y, z, half))

    relayed = {0: [], 1: [], 2: []}

    def relay_part(part, *chunks):
        dp_far = x * 2 + z_other
        relayed[part].append(chunks)
        for core_of in (core, twin):
            piece_arrived(part, core_of, dp_far, *chunks)
            for k in (2, 1, 3):
                send(piece(part, core_of, dp_far, *chunks), piece(part, core_of, dp_far, *chunks),
                     piece_sem(part, core_of, dp_far, *chunks), device((x + k) % NX, y, z, core))

    def spread_arrived(part):
        locals_[part].wait()
        for k in range(NX):
            for core_of in (core, twin):
                if not (k == 0 and core_of is core):
                    piece_arrived(part, core_of, ((x + k) % NX) * 2 + z_hi)

    def relay_arrived(part, *chunks):
        for k in range(1, NX):
            for core_of in (core, twin):
                piece_arrived(part, core_of, ((x + k) % NX) * 2 + z_other, *chunks)

    def token_view(block, distance, way):
        if distance == STEPS:
            return token_all.at[block, :, pl.ds((1 - way) * (D // 2), D // 2 + (1 - way) * META)]
        return token_all.at[block]

    def token_send(group, way):
        sign = 1 - 2 * way
        block = (z + NZ - sign * STRIDE * group) % NZ
        for hop in range(STRIDE, 0, -1):
            distance = STRIDE * group + hop
            send(token_view(block, distance, way), token_view(block, distance, way),
                 token_sem.at[way, distance - 1], along[sign * hop])

    def token_group(group):
        for way in range(2):
            if group == 0:
                token_send(0, way)
                continue
            sign = 1 - 2 * way
            block = (z + NZ - sign * STRIDE * group) % NZ
            arrived(token_view(block, STRIDE * group, way), token_sem.at[way, STRIDE * group - 1])
            if group < STEPS // STRIDE:
                token_send(group, way)
        if group == STEPS // STRIDE:
            for way in range(2):
                for distance in [at for at in range(1, STEPS) if at % STRIDE]:
                    block = (z + NZ - (1 - 2 * way) * distance) % NZ
                    arrived(token_view(block, distance, way), token_sem.at[way, distance - 1])

    def dispatch():
        turned = token_all[:, :, D:].reshape(COL, META).astype(F32).T
        chosen = turned[0:TOP]
        gate = turned[TOP:2 * TOP] + turned[2 * TOP:3 * TOP] + turned[3 * TOP:4 * TOP]
        lane64 = lax.broadcasted_iota(jnp.int32, (64, COL), 1)
        row8 = lax.broadcasted_iota(jnp.int32, (8, COL), 0)
        match = jnp.zeros((8, COL), F32)
        hits, weight = [], []
        for k in range(NY):
            wanted = place_ref[2 * (((y + k) % NY) * ZLO + z_lo) + z_hi].astype(F32)
            same = jnp.where(chosen == wanted, 1.0, 0.0)
            hits.append(jnp.sum(same, axis=0, keepdims=True))
            weight.append(jnp.sum(same * gate, axis=0, keepdims=True))
            match = match + jnp.where(row8 == k, hits[k], 0.0)
        before = lax.broadcasted_iota(jnp.int32, (COL, COL), 0)
        after = lax.broadcasted_iota(jnp.int32, (COL, COL), 1)
        earlier = jnp.where((before < after) & (before // ROWS == after // ROWS), 1.0, 0.0).astype(BF16)
        rank = jnp.dot(match.astype(BF16), earlier, preferred_element_type=F32)
        sent_row = lax.broadcasted_iota(jnp.int32, (SEND, COL), 0)
        sent_rank = (sent_row % CAP).astype(F32)
        same_block = sent_row // CAP == lane64 // ROWS
        picks = []
        for k in range(NY):
            picks.append(jnp.where(same_block & (sent_rank == rank[k:k + 1]), hits[k], 0.0))
        pick = jnp.concatenate(picks, axis=0)
        scaled = jnp.concatenate([picks[k] * weight[k] for k in range(NY)], axis=0).T
        high = scaled.astype(BF16)
        pick_hi[...] = high
        pick_lo[...] = (scaled - high.astype(F32)).astype(BF16)
        pick = pick.astype(BF16)
        every = token_all[:, :, 0:D].reshape(COL, D)
        for k in (2, 1, 3, 0):
            moved = jnp.dot(pick[k * SEND:(k + 1) * SEND], every, preferred_element_type=F32).astype(BF16)
            if k == 0:
                rows_all[core, y] = moved
                send(rows_all.at[core, y], rows_all.at[core, y], twin_sem.at[0], device(x, y, z, twin))
            else:
                rows_out[k - 1] = moved
                send(rows_out.at[k - 1], rows_all.at[core, y], rows_sem.at[k], device(x, (y + k) % NY, z, core))

    def count():
        chosen = token_all[:, :, D:].reshape(COL, META).astype(F32).T[0:TOP]
        expert_row = lax.broadcasted_iota(jnp.int32, (64, COL), 0).astype(F32)
        named = jnp.zeros((64, COL), F32)
        for k in range(TOP):
            named = named + jnp.where(chosen[k:k + 1] == expert_row, 1.0, 0.0)
        ours = jnp.where(
            lax.broadcasted_iota(jnp.int32, (8, COL), 1) // (COL // 2) == z_hi, 1.0, 0.0)
        hist_out[...] = lax.dot_general(
            ours, jnp.concatenate([named, jnp.zeros((64, COL), F32)], axis=0),
            (((1,), (1,)), ((), ())), preferred_element_type=F32)
        hist_in[0] = hist_out[...]
        for k in range(NY):
            for index, other in enumerate((core, twin)):
                if k + index > 0:
                    send(hist_out, hist_in.at[2 * k + index], hist_sem.at[2 * k + index],
                         device(x, (y + k) % NY, z, other))

    def exchange_rows():
        for k in (1, 3, 2):
            giver = (y + NY - k) % NY
            arrived(rows_all.at[core, giver], rows_sem.at[k])
            send(rows_all.at[core, giver], rows_all.at[core, giver], twin_sem.at[k], device(x, y, z, twin))
        for k in range(NY):
            arrived(rows_all.at[twin, (y + NY - k) % NY], twin_sem.at[k])

    def first_products():
        for part in range(2):
            spread_arrived(part)
            for chunks in relayed[part]:
                relay_arrived(part, *chunks)
        for plane in range(2):
            rows = rows_all[plane].reshape(NY * SEND, D)
            a = jnp.dot(rows, matrix[0].reshape(D, HALF), preferred_element_type=F32)
            b = jnp.dot(rows, matrix[1].reshape(D, HALF), preferred_element_type=F32)
            hidden[plane] = (a / (1.0 + jnp.exp(-a)) * b).astype(BF16)

    nt = (((1,), (1,)), ((), ()))

    def down_products(chunk):
        if chunk == 0:
            spread_arrived(2)
        relay_arrived(2, chunk, 1)
        down = down_all[chunk].reshape(WIDTH, HALF)
        cross_out[chunk] = lax.dot_general(hidden[twin], down, nt, preferred_element_type=F32).astype(BF16)
        send(cross_out.at[chunk], cross_in.at[chunk], cross_sem.at[chunk], device(x, y, z, twin))
        own_sum[chunk] = lax.dot_general(hidden[core], down, nt, preferred_element_type=F32)

    def rows_back(chunk):
        arrived(cross_in.at[chunk], cross_sem.at[chunk])
        total = (own_sum[chunk] + cross_in[chunk].astype(F32)).astype(BF16)
        back_out[chunk] = total.reshape(NY, SEND, WIDTH)
        for k in (2, 1, 3):
            giver = (y + NY - k) % NY
            send(back_out.at[chunk, giver], back_in.at[chunk, k], back_sem.at[chunk, k], device(x, giver, z, core))
        back_in[chunk, 0] = back_out[chunk, y]

    def next_stop(chunk, distance):
        return max(stop for stop in STOPS[chunk] if stop < distance)

    def reach(chunk, way):
        return STEPS if chunk % 2 == way else STEPS - 1

    def block_of(way, distance):
        return (z + NZ + (1 - 2 * way) * distance) % NZ

    def ring_send(chunk, way, distance):
        hop = distance - next_stop(chunk, distance)
        send(ring_out.at[way, distance - 1, chunk], ring_in.at[way, distance - 1, chunk],
             ring_sem.at[way, distance - 1, chunk], along[(1 - 2 * way) * hop])

    def ring_sum(chunk, way, distance):
        total = mixing[chunk, block_of(way, distance)] if distance else 0.0
        for farther in range(1, reach(chunk, way) + 1):
            if next_stop(chunk, farther) == distance:
                arrived(ring_in.at[way, farther - 1, chunk], ring_sem.at[way, farther - 1, chunk])
                total = total + ring_in[way, farther - 1, chunk].astype(F32)
        return total

    def mix(chunk):
        for k in (1, 3, 2):
            arrived(back_in.at[chunk, k], back_sem.at[chunk, k])
        got = back_in[chunk].reshape(NY * SEND, WIDTH)
        total = jnp.dot(pick_hi[...], got, preferred_element_type=F32)
        total = total + jnp.dot(pick_lo[...], got, preferred_element_type=F32)
        mixing[chunk] = total.reshape(NZ, ROWS, WIDTH)
        for distance in range(STEPS, 0, -1):
            for way in range(2):
                if distance <= reach(chunk, way) and distance not in STOPS[chunk]:
                    ring_out[way, distance - 1, chunk] = mixing[chunk, block_of(way, distance)].astype(BF16)
                    ring_send(chunk, way, distance)

    def ring_step(chunk, step):
        distance = STOPS[chunk][step]
        if distance == 0:
            return finish(chunk)
        for way in (chunk % 2, 1 - chunk % 2):
            ring_out[way, distance - 1, chunk] = ring_sum(chunk, way, distance).astype(BF16)
            ring_send(chunk, way, distance)

    def finish(chunk):
        total = mixing[chunk, z] + ring_sum(chunk, 0, 0) + ring_sum(chunk, 1, 0)
        lane = lax.broadcasted_iota(jnp.int32, (ROWS, PIECE), 1)
        for p in range(D // PIECE):
            first = p // CHUNKS * PIECE
            moved = total[:, first:first + PIECE]
            shift = (chunk - p % CHUNKS) % CHUNKS * PART
            if shift:
                moved = pltpu.roll(moved, shift, 1)
            at = pl.ds(p * PIECE, PIECE)
            if chunk == 0:
                final[:, at] = moved
            elif chunk < CHUNKS - 1:
                final[:, at] = jnp.where(lane // PART == chunk, moved, final[:, at])
            else:
                mixed_ref[:, at] = jnp.where(lane // PART == chunk, moved, final[:, at]).astype(BF16)

    stages = {
        "p": crossed, "d": dispatch, "w": exchange_rows, "a": first_products, "h": count,
        "t": token_group, "c": cross_part, "s": spread_part, "r": relay_part,
        "C": lambda chunk: cross_part(2, chunk, 1), "R": lambda chunk: relay_part(2, chunk, 1),
        "Y": down_products, "b": rows_back, "m": mix,
    }
    for event in ORDER:
        stages[event[0]](*[int(digit) for digit in event[1:]])
    for slot in range(CHUNKS + 7):
        for late in range(8):
            chunk = slot - late
            if 0 <= chunk < CHUNKS:
                if late < 4:
                    stages["RYbm"[late]](chunk)
                elif late - 4 < len(STOPS[chunk]) - (chunk == CHUNKS - 1):
                    ring_step(chunk, late - 4)
    finish(CHUNKS - 1)

    for index in range(1, 2 * NY):
        arrived(hist_in.at[index], hist_sem.at[index])
    counts = jnp.sum(hist_in[...], axis=0)
    lane = lax.broadcasted_iota(jnp.int32, (8, 128), 1)
    mine = jnp.sum(jnp.where(lane == engine_ref[ep], counts, 0.0), axis=1, keepdims=True)
    load_ref[...] = mine[0:1] / (ROWS * TOP)
    for copy in sends:
        if not any(copy is other for other in waited):
            copy.wait_send()


def on_device(trainer_weights, trainer_place, engine_place, tokens, routes, gates):
    vmem = pl.BlockSpec(memory_space=pltpu.VMEM)
    dma = pltpu.SemaphoreType.DMA
    return pl.pallas_call(
        layer_kernel,
        out_shape=(
            jax.ShapeDtypeStruct((ROWS, D), BF16),
            jax.ShapeDtypeStruct((1, 1), F32),
        ),
        in_specs=[pl.BlockSpec(memory_space=pl.ANY)] * 6,
        out_specs=(vmem, vmem),
        scratch_shapes=[
            pltpu.VMEM((2, 16, CHUNKS, PART, HALF), BF16),
            pltpu.VMEM((CHUNKS, 16, PART, HALF), BF16),
            pltpu.VMEM((NZ, ROWS, D + META), BF16),
            pltpu.VMEM((NY - 1, SEND, D), BF16),
            pltpu.VMEM((2, NY, SEND, D), BF16),
            pltpu.VMEM((COL, NY * SEND), BF16),
            pltpu.VMEM((COL, NY * SEND), BF16),
            pltpu.VMEM((2, NY * SEND, HALF), BF16),
            pltpu.VMEM((CHUNKS, NY * SEND, WIDTH), BF16),
            pltpu.VMEM((CHUNKS, NY * SEND, WIDTH), BF16),
            pltpu.VMEM((CHUNKS, NY * SEND, WIDTH), F32),
            pltpu.VMEM((CHUNKS, NY, SEND, WIDTH), BF16),
            pltpu.VMEM((CHUNKS, NY, SEND, WIDTH), BF16),
            pltpu.VMEM((CHUNKS, NZ, ROWS, WIDTH), F32),
            pltpu.VMEM((2, STEPS, CHUNKS, ROWS, WIDTH), BF16),
            pltpu.VMEM((2, STEPS, CHUNKS, ROWS, WIDTH), BF16),
            pltpu.VMEM((ROWS, D), F32),
            pltpu.VMEM((8, 128), F32),
            pltpu.VMEM((2 * NY, 8, 128), F32),
            pltpu.SMEM((NZ * NY,), jnp.int32),
            pltpu.SMEM((NZ * NY,), jnp.int32),
            pltpu.VMEM((TOP, ROWS), jnp.int32),
            pltpu.VMEM((TOP, ROWS), F32),
            dma((8,)),
            dma((192,)),
            dma((3, 16, CHUNKS)),
            dma((2, STEPS)),
            dma((NY,)),
            dma((NY,)),
            dma((CHUNKS,)),
            dma((CHUNKS, NY)),
            dma((2, STEPS, CHUNKS)),
            dma((2 * NY,)),
        ],
        compiler_params=pltpu.CompilerParams(
            collective_id=0, has_side_effects=True, vmem_limit_bytes=60 * 2**20
        ),
    )(trainer_place, engine_place, trainer_weights[0].reshape(2, CHUNKS, PART, 3 * FF), tokens, routes.T, gates.T)


def solution(mesh):
    in_specs = (
        P("ep", None, "dp", None),
        P(),
        P(),
        P(("dp", "ep"), None),
        P(("dp", "ep"), None),
        P(("dp", "ep"), None),
    )
    out_specs = (P(("dp", "ep"), None), P("dp", "ep"))
    return jax.shard_map(
        on_device, mesh=mesh, in_specs=in_specs, out_specs=out_specs, check_vma=False
    )
```

```python
import functools

import jax
import jax.numpy as jnp
from jax import lax
from jax.experimental import pallas as pl
from jax.experimental.pallas import tpu as pltpu
from jax.sharding import PartitionSpec as P

MESH = pl.DeviceIdType.MESH
NX, NY, NZ = 4, 4, 16
ZLO = 8
D = 2048
FF = 768
HALF = FF // 2
ROWS = 16
TOP = 8
CAP = 4
PIECE = 128
COL = NZ * ROWS
SEND = NZ * CAP
CHUNKS = 4
WIDTH = D // CHUNKS
PART = PIECE // CHUNKS
STEPS = NZ // 2
BF16, F32 = jnp.bfloat16, jnp.float32
META = 128
ORDER = (
    "t0", "c0", "s0", "s1", "s2", "t1", "t2", "c1", "t3", "r0", "t4",
    "d", "r1", "C0", "C1", "C2", "C3", "w", "a", "h",
)
STRIDE = 2
STOPS = ((6, 4, 2, 0), (6, 4, 2, 0), (6, 4, 2, 0), (5, 2, 0))


def device(x, y, z, core):
    return (x * 2 + z // ZLO, (y * ZLO + z % ZLO) * 2 + core)


def layer_kernel(
    place_any, engine_any, weights, tokens_ref, routes_any, gates_any,
    mixed_ref, load_ref,
    matrix, down_all, token_all, rows_out, rows_all, pick_hi, pick_lo, hidden,
    cross_out, cross_in, own_sum, back_out, back_in, mixing, ring_out, ring_in, final,
    hist_out, hist_in, place_ref, engine_ref, routes_ref, gates_ref,
    local_sem, send_sem, matrix_sem, token_sem, rows_sem, twin_sem,
    cross_sem, back_sem, ring_sem, hist_sem,
):
    dp, ep = lax.axis_index("dp"), lax.axis_index("ep")
    x, z_hi = dp // 2, dp % 2
    y, z_lo, core = ep // 16, (ep // 2) % ZLO, ep % 2
    z = z_hi * ZLO + z_lo
    far = (z + ZLO) % NZ
    z_other = 1 - z_hi
    twin = 1 - core

    fetches = [
        pltpu.make_async_copy(src, dst, local_sem.at[3 + index])
        for index, (src, dst) in enumerate((
            (routes_any, routes_ref), (gates_any, gates_ref), (tokens_ref, token_all.at[z, :, pl.ds(0, D)]),
            (place_any, place_ref), (engine_any, engine_ref)))
    ]
    for copy in fetches:
        copy.start()
    partners = [device(x, y, far, other) for other in (core, twin)]
    for k in range(NX):
        for other in (core, twin):
            if not (k == 0 and other is core):
                partners.append(device((x + k) % NX, y, z, other))
    for k in range(1, NY):
        for other in (core, twin):
            partners.append(device(x, (y + k) % NY, z, other))
    along = {step: device(x, y, (z + NZ + step) % NZ, core) for step in (1, 2, 3, -1, -2, -3)}
    partners += list(along.values())
    barrier = pltpu.get_barrier_semaphore()
    for partner in partners:
        pl.semaphore_signal(barrier, inc=1, device_id=partner, device_id_type=MESH)
    for copy in fetches:
        copy.wait()
    gate_parts, rest = [], gates_ref[...]
    for _ in range(3):
        gate_parts.append(rest.astype(BF16).astype(F32))
        rest = rest - gate_parts[-1]
    facts = jnp.concatenate([routes_ref[...].astype(F32)] + gate_parts, axis=0)
    facts = jnp.concatenate([facts, jnp.zeros((4 * TOP, META - ROWS), F32)], axis=1)
    facts = jnp.concatenate([facts, jnp.zeros((META - 4 * TOP, META), F32)], axis=0)
    token_all[z, :, D:] = facts.T[0:ROWS].astype(BF16)
    pl.semaphore_wait(barrier, len(partners))

    sends, waited = [], []

    def send(src, dst, sem, to):
        copy = pltpu.make_async_remote_copy(
            src_ref=src, dst_ref=dst, send_sem=send_sem.at[len(sends)], recv_sem=sem,
            device_id=to, device_id_type=MESH,
        )
        copy.start()
        sends.append(copy)
        return copy

    def arrived(ref, sem):
        pltpu.make_async_copy(ref, ref, sem).wait()

    def piece(part, core_of, dp_of, first=0, count=CHUNKS):
        source = core_of * 8 + dp_of
        if part < 2:
            return matrix.at[part, source, pl.ds(first, count)]
        return down_all.at[pl.ds(first, count), source]

    def piece_sem(part, core_of, dp_of, first=0, count=CHUNKS):
        return matrix_sem.at[part, core_of * 8 + dp_of, first]

    def own_piece(slot, part, half, first=0, count=CHUNKS):
        columns = pl.ds(pl.multiple_of(part * FF + half * HALF, 128), HALF)
        return weights.at[slot, pl.ds(first, count), :, columns]

    def piece_arrived(*at):
        arrived(piece(*at), piece_sem(*at))

    crossing = {}

    def crossed(part, *chunks):
        for copy in crossing.pop((part,) + chunks):
            copy.wait_send()
            waited.append(copy)

    def cross_part(part, *chunks):
        crossing[(part,) + chunks] = []
        for half in (core, twin):
            crossing[(part,) + chunks].append(send(own_piece(z_other, part, half, *chunks), piece(part, core, dp, *chunks),
                 piece_sem(part, core, dp, *chunks), device(x, y, far, half)))

    locals_ = {}

    def spread_part(part):
        locals_[part] = pltpu.make_async_copy(
            own_piece(z_hi, part, core), piece(part, core, dp), local_sem.at[part])
        locals_[part].start()
        for half in (core, twin):
            for k in (1, 3, 2, 0):
                if k == 0 and half is core:
                    continue
                send(own_piece(z_hi, part, half), piece(part, core, dp),
                     piece_sem(part, core, dp), device((x + k) % NX, y, z, half))

    relayed = {0: [], 1: [], 2: []}

    def relay_part(part, *chunks):
        dp_far = x * 2 + z_other
        relayed[part].append(chunks)
        for core_of in (core, twin):
            piece_arrived(part, core_of, dp_far, *chunks)
            for k in (2, 1, 3):
                send(piece(part, core_of, dp_far, *chunks), piece(part, core_of, dp_far, *chunks),
                     piece_sem(part, core_of, dp_far, *chunks), device((x + k) % NX, y, z, core))

    def spread_arrived(part):
        locals_[part].wait()
        for k in range(NX):
            for core_of in (core, twin):
                if not (k == 0 and core_of is core):
                    piece_arrived(part, core_of, ((x + k) % NX) * 2 + z_hi)

    def relay_arrived(part, *chunks):
        for k in range(1, NX):
            for core_of in (core, twin):
                piece_arrived(part, core_of, ((x + k) % NX) * 2 + z_other, *chunks)

    def token_view(block, distance, way):
        if distance == STEPS:
            return token_all.at[block, :, pl.ds((1 - way) * (D // 2), D // 2 + (1 - way) * META)]
        return token_all.at[block]

    def token_send(group, way):
        sign = 1 - 2 * way
        block = (z + NZ - sign * STRIDE * group) % NZ
        for hop in range(STRIDE, 0, -1):
            distance = STRIDE * group + hop
            send(token_view(block, distance, way), token_view(block, distance, way),
                 token_sem.at[way, distance - 1], along[sign * hop])

    def token_group(group):
        for way in range(2):
            if group == 0:
                token_send(0, way)
                continue
            sign = 1 - 2 * way
            block = (z + NZ - sign * STRIDE * group) % NZ
            arrived(token_view(block, STRIDE * group, way), token_sem.at[way, STRIDE * group - 1])
            if group < STEPS // STRIDE:
                token_send(group, way)
        if group == STEPS // STRIDE:
            for way in range(2):
                for distance in [at for at in range(1, STEPS) if at % STRIDE]:
                    block = (z + NZ - (1 - 2 * way) * distance) % NZ
                    arrived(token_view(block, distance, way), token_sem.at[way, distance - 1])

    def dispatch():
        turned = token_all[:, :, D:].reshape(COL, META).astype(F32).T
        chosen = turned[0:TOP]
        gate = turned[TOP:2 * TOP] + turned[2 * TOP:3 * TOP] + turned[3 * TOP:4 * TOP]
        lane64 = lax.broadcasted_iota(jnp.int32, (64, COL), 1)
        row8 = lax.broadcasted_iota(jnp.int32, (8, COL), 0)
        match = jnp.zeros((8, COL), F32)
        hits, weight = [], []
        for k in range(NY):
            wanted = place_ref[2 * (((y + k) % NY) * ZLO + z_lo) + z_hi].astype(F32)
            same = jnp.where(chosen == wanted, 1.0, 0.0)
            hits.append(jnp.sum(same, axis=0, keepdims=True))
            weight.append(jnp.sum(same * gate, axis=0, keepdims=True))
            match = match + jnp.where(row8 == k, hits[k], 0.0)
        before = lax.broadcasted_iota(jnp.int32, (COL, COL), 0)
        after = lax.broadcasted_iota(jnp.int32, (COL, COL), 1)
        earlier = jnp.where((before < after) & (before // ROWS == after // ROWS), 1.0, 0.0).astype(BF16)
        rank = jnp.dot(match.astype(BF16), earlier, preferred_element_type=F32)
        sent_row = lax.broadcasted_iota(jnp.int32, (SEND, COL), 0)
        sent_rank = (sent_row % CAP).astype(F32)
        same_block = sent_row // CAP == lane64 // ROWS
        picks = []
        for k in range(NY):
            picks.append(jnp.where(same_block & (sent_rank == rank[k:k + 1]), hits[k], 0.0))
        pick = jnp.concatenate(picks, axis=0)
        pick = pick.astype(BF16)
        every = token_all[:, :, 0:D].reshape(COL, D)
        for k in (2, 1, 3, 0):
            moved = jnp.dot(pick[k * SEND:(k + 1) * SEND], every, preferred_element_type=F32).astype(BF16)
            if k == 0:
                rows_all[core, y] = moved
                send(rows_all.at[core, y], rows_all.at[core, y], twin_sem.at[0], device(x, y, z, twin))
            else:
                rows_out[k - 1] = moved
                send(rows_out.at[k - 1], rows_all.at[core, y], rows_sem.at[k], device(x, (y + k) % NY, z, core))
        scaled = jnp.concatenate([picks[k] * weight[k] for k in range(NY)], axis=0).T
        high = scaled.astype(BF16)
        pick_hi[...] = high
        pick_lo[...] = (scaled - high.astype(F32)).astype(BF16)

    def count():
        chosen = token_all[:, :, D:].reshape(COL, META).astype(F32).T[0:TOP]
        expert_row = lax.broadcasted_iota(jnp.int32, (64, COL), 0).astype(F32)
        named = jnp.zeros((64, COL), F32)
        for k in range(TOP):
            named = named + jnp.where(chosen[k:k + 1] == expert_row, 1.0, 0.0)
        ours = jnp.where(
            lax.broadcasted_iota(jnp.int32, (8, COL), 1) // (COL // 2) == z_hi, 1.0, 0.0)
        hist_out[...] = lax.dot_general(
            ours, jnp.concatenate([named, jnp.zeros((64, COL), F32)], axis=0),
            (((1,), (1,)), ((), ())), preferred_element_type=F32)
        hist_in[0] = hist_out[...]
        for k in range(NY):
            for index, other in enumerate((core, twin)):
                if k + index > 0:
                    send(hist_out, hist_in.at[2 * k + index], hist_sem.at[2 * k + index],
                         device(x, (y + k) % NY, z, other))

    def exchange_rows():
        for k in (1, 3, 2):
            giver = (y + NY - k) % NY
            arrived(rows_all.at[core, giver], rows_sem.at[k])
            send(rows_all.at[core, giver], rows_all.at[core, giver], twin_sem.at[k], device(x, y, z, twin))
        for k in range(NY):
            arrived(rows_all.at[twin, (y + NY - k) % NY], twin_sem.at[k])

    def first_products():
        for part in range(2):
            spread_arrived(part)
            for chunks in relayed[part]:
                relay_arrived(part, *chunks)
        for plane in range(2):
            rows = rows_all[plane].reshape(NY * SEND, D)
            a = jnp.dot(rows, matrix[0].reshape(D, HALF), preferred_element_type=F32)
            b = jnp.dot(rows, matrix[1].reshape(D, HALF), preferred_element_type=F32)
            hidden[plane] = (a / (1.0 + jnp.exp(-a)) * b).astype(BF16)

    nt = (((1,), (1,)), ((), ()))

    def down_products(chunk):
        if chunk == 0:
            spread_arrived(2)
        relay_arrived(2, chunk, 1)
        down = down_all[chunk].reshape(WIDTH, HALF)
        cross_out[chunk] = lax.dot_general(hidden[twin], down, nt, preferred_element_type=F32).astype(BF16)
        send(cross_out.at[chunk], cross_in.at[chunk], cross_sem.at[chunk], device(x, y, z, twin))
        own_sum[chunk] = lax.dot_general(hidden[core], down, nt, preferred_element_type=F32)

    def rows_back(chunk):
        arrived(cross_in.at[chunk], cross_sem.at[chunk])
        total = (own_sum[chunk] + cross_in[chunk].astype(F32)).astype(BF16)
        back_out[chunk] = total.reshape(NY, SEND, WIDTH)
        for k in (2, 1, 3):
            giver = (y + NY - k) % NY
            send(back_out.at[chunk, giver], back_in.at[chunk, k], back_sem.at[chunk, k], device(x, giver, z, core))
        back_in[chunk, 0] = back_out[chunk, y]

    def next_stop(chunk, distance):
        return max(stop for stop in STOPS[chunk] if stop < distance)

    def reach(chunk, way):
        return STEPS if chunk % 2 == way else STEPS - 1

    def block_of(way, distance):
        return (z + NZ + (1 - 2 * way) * distance) % NZ

    def ring_send(chunk, way, distance):
        hop = distance - next_stop(chunk, distance)
        send(ring_out.at[way, distance - 1, chunk], ring_in.at[way, distance - 1, chunk],
             ring_sem.at[way, distance - 1, chunk], along[(1 - 2 * way) * hop])

    def ring_sum(chunk, way, distance):
        total = mixing[chunk, block_of(way, distance)] if distance else 0.0
        for farther in range(1, reach(chunk, way) + 1):
            if next_stop(chunk, farther) == distance:
                arrived(ring_in.at[way, farther - 1, chunk], ring_sem.at[way, farther - 1, chunk])
                total = total + ring_in[way, farther - 1, chunk].astype(F32)
        return total

    def mix(chunk):
        for k in (1, 3, 2):
            arrived(back_in.at[chunk, k], back_sem.at[chunk, k])
        got = back_in[chunk].reshape(NY * SEND, WIDTH)
        total = jnp.dot(pick_hi[...], got, preferred_element_type=F32)
        total = total + jnp.dot(pick_lo[...], got, preferred_element_type=F32)
        mixing[chunk] = total.reshape(NZ, ROWS, WIDTH)
        for distance in range(STEPS, 0, -1):
            for way in range(2):
                if distance <= reach(chunk, way) and distance not in STOPS[chunk]:
                    ring_out[way, distance - 1, chunk] = mixing[chunk, block_of(way, distance)].astype(BF16)
                    ring_send(chunk, way, distance)

    def ring_step(chunk, step):
        distance = STOPS[chunk][step]
        if distance == 0:
            return finish(chunk)
        for way in (chunk % 2, 1 - chunk % 2):
            ring_out[way, distance - 1, chunk] = ring_sum(chunk, way, distance).astype(BF16)
            ring_send(chunk, way, distance)

    def finish(chunk):
        total = mixing[chunk, z] + ring_sum(chunk, 0, 0) + ring_sum(chunk, 1, 0)
        lane = lax.broadcasted_iota(jnp.int32, (ROWS, PIECE), 1)
        for p in range(D // PIECE):
            first = p // CHUNKS * PIECE
            moved = total[:, first:first + PIECE]
            shift = (chunk - p % CHUNKS) % CHUNKS * PART
            if shift:
                moved = pltpu.roll(moved, shift, 1)
            at = pl.ds(p * PIECE, PIECE)
            if chunk == 0:
                final[:, at] = moved
            elif chunk < CHUNKS - 1:
                final[:, at] = jnp.where(lane // PART == chunk, moved, final[:, at])
            else:
                mixed_ref[:, at] = jnp.where(lane // PART == chunk, moved, final[:, at]).astype(BF16)

    stages = {
        "p": crossed, "d": dispatch, "w": exchange_rows, "a": first_products, "h": count,
        "t": token_group, "c": cross_part, "s": spread_part, "r": relay_part,
        "C": lambda chunk: cross_part(2, chunk, 1), "R": lambda chunk: relay_part(2, chunk, 1),
        "Y": down_products, "b": rows_back, "m": mix,
    }
    for event in ORDER:
        stages[event[0]](*[int(digit) for digit in event[1:]])
    for slot in range(CHUNKS + 7):
        for late in range(8):
            chunk = slot - late
            if 0 <= chunk < CHUNKS:
                if late < 4:
                    stages["RYbm"[late]](chunk)
                elif late - 4 < len(STOPS[chunk]) - (chunk == CHUNKS - 1):
                    ring_step(chunk, late - 4)
    finish(CHUNKS - 1)

    for index in range(1, 2 * NY):
        arrived(hist_in.at[index], hist_sem.at[index])
    counts = jnp.sum(hist_in[...], axis=0)
    lane = lax.broadcasted_iota(jnp.int32, (8, 128), 1)
    mine = jnp.sum(jnp.where(lane == engine_ref[ep], counts, 0.0), axis=1, keepdims=True)
    load_ref[...] = mine[0:1] / (ROWS * TOP)
    for copy in sends:
        if not any(copy is other for other in waited):
            copy.wait_send()


def on_device(trainer_weights, trainer_place, engine_place, tokens, routes, gates):
    vmem = pl.BlockSpec(memory_space=pltpu.VMEM)
    dma = pltpu.SemaphoreType.DMA
    return pl.pallas_call(
        layer_kernel,
        out_shape=(
            jax.ShapeDtypeStruct((ROWS, D), BF16),
            jax.ShapeDtypeStruct((1, 1), F32),
        ),
        in_specs=[pl.BlockSpec(memory_space=pl.ANY)] * 6,
        out_specs=(vmem, vmem),
        scratch_shapes=[
            pltpu.VMEM((2, 16, CHUNKS, PART, HALF), BF16),
            pltpu.VMEM((CHUNKS, 16, PART, HALF), BF16),
            pltpu.VMEM((NZ, ROWS, D + META), BF16),
            pltpu.VMEM((NY - 1, SEND, D), BF16),
            pltpu.VMEM((2, NY, SEND, D), BF16),
            pltpu.VMEM((COL, NY * SEND), BF16),
            pltpu.VMEM((COL, NY * SEND), BF16),
            pltpu.VMEM((2, NY * SEND, HALF), BF16),
            pltpu.VMEM((CHUNKS, NY * SEND, WIDTH), BF16),
            pltpu.VMEM((CHUNKS, NY * SEND, WIDTH), BF16),
            pltpu.VMEM((CHUNKS, NY * SEND, WIDTH), F32),
            pltpu.VMEM((CHUNKS, NY, SEND, WIDTH), BF16),
            pltpu.VMEM((CHUNKS, NY, SEND, WIDTH), BF16),
            pltpu.VMEM((CHUNKS, NZ, ROWS, WIDTH), F32),
            pltpu.VMEM((2, STEPS, CHUNKS, ROWS, WIDTH), BF16),
            pltpu.VMEM((2, STEPS, CHUNKS, ROWS, WIDTH), BF16),
            pltpu.VMEM((ROWS, D), F32),
            pltpu.VMEM((8, 128), F32),
            pltpu.VMEM((2 * NY, 8, 128), F32),
            pltpu.SMEM((NZ * NY,), jnp.int32),
            pltpu.SMEM((NZ * NY,), jnp.int32),
            pltpu.VMEM((TOP, ROWS), jnp.int32),
            pltpu.VMEM((TOP, ROWS), F32),
            dma((8,)),
            dma((192,)),
            dma((3, 16, CHUNKS)),
            dma((2, STEPS)),
            dma((NY,)),
            dma((NY,)),
            dma((CHUNKS,)),
            dma((CHUNKS, NY)),
            dma((2, STEPS, CHUNKS)),
            dma((2 * NY,)),
        ],
        compiler_params=pltpu.CompilerParams(
            collective_id=0, has_side_effects=True, vmem_limit_bytes=60 * 2**20
        ),
    )(trainer_place, engine_place, trainer_weights[0].reshape(2, CHUNKS, PART, 3 * FF), tokens, routes.T, gates.T)


def solution(mesh):
    in_specs = (
        P("ep", None, "dp", None),
        P(),
        P(),
        P(("dp", "ep"), None),
        P(("dp", "ep"), None),
        P(("dp", "ep"), None),
    )
    out_specs = (P(("dp", "ep"), None), P("dp", "ep"))
    return jax.shard_map(
        on_device, mesh=mesh, in_specs=in_specs, out_specs=out_specs, check_vma=False
    )
```
